32 devices in a mesh: snap: 2 (over y), gx: 4 (over z), gy: 2 (over x), gz: 2 (over core).
Axes of the slice: x: 2, y: 2, z: 4, core: 2. Of those that a mesh axis runs over, the one named last changes fastest.
Arguments:
- core_tensor: float32 [3, 512, 256, 128], P(None, ('snap', 'gx'), ('gy', 'gz')), parts along dimension 1, may hold values from -6 to 6
- first_factor: float32 [128, 256], P(('snap', 'gx')), parts along dimension 0, may hold values from -0.375 to 0.375
- second_factor: float32 [384, 256], P(('snap', 'gy')), parts along dimension 0, may hold values from -0.375 to 0.375
- third_factor: float32 [512, 128], P(('snap', 'gz')), parts along dimension 0, may hold values from -0.5 to 0.5
Outputs:
- vorticity: bfloat16 [3, 128, 192, 256], P(None, ('snap', 'gx'), 'gy', 'gz'), parts along dimension 1
- q_criterion: bfloat16 [128, 192, 256], P(('snap', 'gx'), 'gy', 'gz'), parts along dimension 0
The draws below stay inside these ranges and needn't reach their ends.
There are 2 independent parts, one for each index of `snap`. The reference program is written for one: setup_inputs(seed, part) draws one part's arguments, and reference() takes and returns one part's arrays. A program takes and returns all parts, laid end to end along the dimension named above; each array names one. Nothing has to cross between parts.
All inputs are finite; a program needn't handle non-finite values.
Results may differ from the reference program's by a relative error of at most 0.0056.
Values may be sent and summed in bfloat16 or wider, within the bound.
No kernel may reach another device: no remote copies, remote signals or barrier semaphores. Data moves between devices by JAX's collectives and lax.ppermute only.
A program may use at most 64 MiB of HBM per device.

```python
import jax
import jax.numpy as jnp
from jax import lax

R1 = 256
R2 = 256
R3 = 128
CX = 16
NX = 64
NY = 192
NZ = 256
N_GX = 4


def block_scale(stream_key, shape, cuts, low, high):
    gain = 1.0
    for position, shards_of in cuts:
        heights = jax.random.uniform(jax.random.fold_in(jax.random.fold_in(stream_key, 6), position), (shards_of,), jnp.float32, low / len(cuts), high / len(cuts))
        gain = gain * jnp.repeat(jnp.exp(heights), shape[position] // shards_of).reshape((-1,) + (1,) * (len(shape) - 1 - position))
    return gain


def centred(rng, shape, spread, most, cuts=(), held_as=jnp.bfloat16):
    drawn = jax.random.normal(rng, shape, jnp.float32) * spread
    if len(cuts) > 0:
        drawn = block_scale(rng, shape, cuts, -0.22, 0.18) * drawn
    return jnp.clip(drawn, min=-most, max=most).astype(held_as)


def setup_inputs(seed: int = 0, part: int = 0) -> dict:
    streams_of = jax.random.split(jax.random.key(seed), 5)
    own_keys = jax.random.split(jax.random.fold_in(streams_of[4], part), 5)
    core_tensor = centred(own_keys[0], (3, R1, R2, R3), 1.0, 6.0, ((1, 4), (2, 4)), jnp.float32)
    first_factor = centred(own_keys[1], (NX, R1), R1 ** -0.5, 0.375, ((0, 4),), jnp.float32)
    second_factor = centred(own_keys[2], (NY, R2), R2 ** -0.5, 0.375, ((0, 2),), jnp.float32)
    third_factor = centred(own_keys[3], (NZ, R3), R3 ** -0.5, 0.5, ((0, 2),), jnp.float32)
    return dict(core_tensor=core_tensor, first_factor=first_factor, second_factor=second_factor, third_factor=third_factor)


highest = lax.Precision.HIGHEST


def derivative(extended, direction):
    length = extended.shape[direction]

    def shifted(offset):
        index_list = [slice(None), slice(2, -2), slice(2, -2), slice(2, -2)]
        index_list[direction] = slice(2 + offset, length - 2 + offset)
        return extended[tuple(index_list)]

    return (shifted(-2) - 8.0 * shifted(-1) + 8.0 * shifted(1) - shifted(2)) / 12.0


def invariants(extended):
    along_x = derivative(extended, 1)
    along_y = derivative(extended, 2)
    along_z = derivative(extended, 3)
    curl = jnp.stack([along_y[2] - along_z[1], along_z[0] - along_x[2], along_x[1] - along_y[0]])
    trace_part = along_x[0] * along_x[0] + along_y[1] * along_y[1] + along_z[2] * along_z[2]
    cross_part = along_y[0] * along_x[1] + along_z[0] * along_x[2] + along_z[1] * along_y[2]
    q_value = -0.5 * (trace_part + 2.0 * cross_part)
    return curl.astype(jnp.bfloat16), q_value.astype(jnp.bfloat16)


def reference(core_tensor, first_factor, second_factor, third_factor):
    section_one = jnp.einsum('cabg,xa->cxbg', core_tensor, first_factor, precision=highest)
    section_two = jnp.einsum('cxbg,yb->cxyg', section_one, second_factor, precision=highest)
    velocity = jnp.einsum('cxyg,zg->cxyz', section_two, third_factor, precision=highest).astype(jnp.bfloat16)
    padded = jnp.pad(velocity, ((0, 0), (2, 2), (2, 2), (2, 2)))
    anchor = jnp.zeros((), jnp.int32)

    def one_block(offset):
        extended = lax.dynamic_slice(padded, (anchor, offset, anchor, anchor), (3, CX + 4, NY + 4, NZ + 4))
        return invariants(extended.astype(jnp.float32))

    offsets = jnp.arange(N_GX, dtype=jnp.int32) * CX
    curl_blocks, q_blocks = lax.map(one_block, offsets)
    vorticity = jnp.moveaxis(curl_blocks, 0, 1).reshape(3, NX, NY, NZ)
    q_criterion = q_blocks.reshape(NX, NY, NZ)
    return vorticity, q_criterion
```

```python
import functools

import jax
import jax.numpy as jnp
from jax import lax
from jax.experimental import pallas as pl
from jax.experimental.pallas import tpu as pltpu
from jax.sharding import PartitionSpec as P

f32, bf16 = jnp.float32, jnp.bfloat16
LANES = 128
VMEM_LIMIT = 48 * 2**20


def split(value):
    high = value.astype(bf16)
    return high, (value - high.astype(f32)).astype(bf16)


def dot(left, right):
    return jnp.dot(left, right, preferred_element_type=f32)


def whole(shape):
    return pl.BlockSpec(shape, lambda *_: (0,) * len(shape))


def call(kernel, out_shapes, in_specs, flops, nbytes, scratch=()):
    return pl.pallas_call(
        kernel,
        grid=(1,),
        out_shape=out_shapes,
        in_specs=in_specs,
        out_specs=jax.tree.map(lambda s: whole(s.shape), out_shapes),
        scratch_shapes=scratch,
        compiler_params=pltpu.CompilerParams(vmem_limit_bytes=VMEM_LIMIT),
        cost_estimate=pl.CostEstimate(flops=flops, bytes_accessed=nbytes, transcendentals=0),
    )


def struct(*shape, dtype=f32):
    return jax.ShapeDtypeStruct(shape, dtype)


def expand_first_kernel(a, b, relay, f1, core, mine, theirs, *sends):
    high, low = split(f1[...])
    left = jnp.concatenate([high, high, low], axis=1)
    half = mine.shape[0] // b

    @pl.loop(0, b // 4)
    def _(step):
        for inner in range(2):
            at = step * 4 + inner * 2
            pair = jnp.concatenate(
                [core[pl.ds(at, a, stride=b), :], core[pl.ds(at + 1, a, stride=b), :]], axis=1
            )
            high, low = split(pair)
            out = dot(left, jnp.concatenate([high, low, high], axis=0))
            for i in range(2):
                rows = out[:, i * LANES : (i + 1) * LANES]
                short = pl.ds(pl.multiple_of((at + i) * half, half), half)
                full = pl.ds(pl.multiple_of((at + i) * 2 * half, 2 * half), 2 * half)
                mine[short, :] = rows[:half]
                theirs[short, :] = rows[half : 2 * half]
                block = [rows[2 * half * k : 2 * half * (k + 1)] for k in range(rows.shape[0] // (2 * half))]
                if relay:
                    near, far, cross = sends
                    near[0, full, :] = block[1].astype(bf16)
                    near[1, full, :] = block[3].astype(bf16)
                    far[full, :] = block[2]
                    cross[full, :] = block[3].astype(bf16)
                else:
                    for k, send in enumerate(sends):
                        send[full, :] = block[k + 1].astype(bf16)


def expand_first(c, f1, core, a, b, half, relay):
    n = f1.shape[0] // (2 * half)
    full = struct(b * 2 * half, LANES, dtype=bf16)
    if relay:
        sends = [struct(2, b * 2 * half, LANES, dtype=bf16), struct(b * 2 * half, LANES), full]
    else:
        sends = [full] * (n - 1)
    return call(
        functools.partial(expand_first_kernel, a, b, relay),
        [struct(b * half, LANES)] * 2 + sends,
        [whole(f1.shape), pl.BlockSpec((a * b, LANES), lambda *_: (c, 0))],
        2 * f1.shape[0] * a * b * LANES * 3,
        a * b * LANES * 4 * 2,
    )(f1, core)


def add_kernel(half, mine, theirs, *refs):
    arrived, (mine_out, theirs_out) = refs[:-2], refs[-2:]
    b = mine.shape[0] // half
    total = 0.0
    for ref in arrived:
        total = total + (ref[0] if len(ref.shape) == 3 else ref[...]).astype(f32)
    total = total.reshape(b, 2, half, LANES)
    mine_out[...] = mine[...] + total[:, 0].reshape(b * half, LANES)
    theirs_out[...] = theirs[...] + total[:, 1].reshape(b * half, LANES)


def add(half, mine, theirs, arrived):
    specs = [
        pl.BlockSpec((1, *x.shape[1:]), lambda *_: (0, 0, 0)) if x.ndim == 3 else whole(x.shape)
        for x in arrived
    ]
    return call(
        functools.partial(add_kernel, half),
        [struct(*mine.shape)] * 2,
        [whole(mine.shape)] * 2 + specs,
        mine.size * 8,
        mine.size * 30,
    )(mine, theirs, *arrived)


def expand_second_kernel(half, f2, mine, other, *refs):
    others, out, wide = refs[:-2], refs[-2], refs[-1]
    b = mine.shape[0] // half
    for i, ref in enumerate(others):
        wide[i] = ref[...].astype(f32)
    f2_high, f2_low = split(f2[...])
    y = f2.shape[0]
    for x in range(0, half, 2):
        def columns(ref, length, *index):
            return jnp.concatenate(
                [ref[(*index, pl.ds(x + i, length, stride=half), slice(None))] for i in range(2)], axis=1
            )

        near = jnp.concatenate([columns(mine, b), columns(other, b)], axis=0)
        high, low = split(near)
        far = [columns(wide, 2 * b, i).astype(bf16) for i in range(len(others))]
        every = jnp.concatenate([high, *far], axis=0)
        value = dot(f2_high, every) + dot(f2_low, every) + dot(f2_high[:, : 2 * b], low)
        for i in range(2):
            out[(x + i) * y : (x + i + 1) * y, :] = value[:, i * LANES : (i + 1) * LANES]


def expand_second(half, f2, mine, other, others):
    y = f2.shape[0]
    return call(
        functools.partial(expand_second_kernel, half),
        struct(half * y, LANES),
        [whole(f2.shape), whole(mine.shape), whole(other.shape)] + [whole(x.shape) for x in others],
        2 * y * f2.shape[1] * half * LANES * 3,
        mine.size * 16 + half * y * LANES * 4,
        [pltpu.VMEM((max(len(others), 1), 2 * mine.shape[0], LANES), f32)],
    )(f2, mine, other, *others)


def finish_kernel(half, y, z, core_id, weights, *refs):
    owned, partner, arrived, passed = refs[0:3], refs[3:6], refs[6:9], refs[9:12]
    curl, q, v, along_z = refs[12:]
    w_high, w_low = split(weights[...])
    right = jnp.concatenate([w_high, w_high, w_low], axis=0)
    rows = y + 8
    core = core_id[0]

    def planes(value, count):
        high, low = split(value)
        out = dot(jnp.concatenate([high, low, high], axis=1), right)
        return out.reshape(count, rows, 2 * z)

    def place(c, first, out):
        at = pl.ds(first, out.shape[0])
        v[c, at, 8 : 8 + rows, :] = out[:, :, :z]
        v[c, at, 0:8, :] = out[:, y:, :z]

    for c in range(3):
        for source, slot in ((owned, core), (partner, 1 - core)):
            for part in range(2):
                size = half // 2 * rows
                out = planes(source[c][part * size : (part + 1) * size, :], half // 2)
                first = slot * half + part * (half // 2)
                place(c, first + 2, out)
                along_z[c, pl.ds(first, half // 2), :, :] = out[:, :y, z:]
        place(c, (1 - core) * (2 * half + 2), planes(arrived[c][...].astype(f32), 2))
        place(c, core * (2 * half + 2), planes(passed[c][...].astype(f32), 2))

    def slope(low2, low1, high1, high2):
        return 8.0 * (high1 - low1) - (high2 - low2)

    @pl.loop(0, 2 * half)
    def _(x):
        def dx(c):
            return slope(*(v[c, x + i, 8 : 8 + y, :] for i in (0, 1, 3, 4)))

        def dy(c):
            return slope(*(v[c, x + 2, 6 + i : 6 + i + y, :] for i in (0, 1, 3, 4)))

        def dz(c):
            return along_z[c, x, :, :]

        x1, x2, y0, y2, z0, z1 = dx(1), dx(2), dy(0), dy(2), dz(0), dz(1)
        curl[0, x] = (y2 - z1).astype(bf16)
        curl[1, x] = (z0 - x2).astype(bf16)
        curl[2, x] = (x1 - y0).astype(bf16)
        cross = y0 * x1 + z0 * x2 + z1 * y2
        x0, y1, z2 = dx(0), dy(1), dz(2)
        trace = x0 * x0 + y1 * y1 + z2 * z2
        q[x] = (-0.5 * (trace + 2.0 * cross)).astype(bf16)


def finish(half, y, z, core_id, weights, owned, partner, arrived, passed):
    arrays = [*owned, *partner, *arrived, *passed]
    rows = y + 8
    return call(
        functools.partial(finish_kernel, half, y, z),
        [struct(3, 2 * half, y, z, dtype=bf16), struct(2 * half, y, z, dtype=bf16)],
        [pl.BlockSpec(memory_space=pltpu.SMEM), whole(weights.shape)] + [whole(x.shape) for x in arrays],
        2 * 3 * (2 * half + 4) * rows * LANES * 2 * z * 3,
        3 * (2 * half + 4) * rows * LANES * 4,
        [pltpu.VMEM((3, 2 * half + 4, y + 16, z), f32), pltpu.VMEM((3, 2 * half, y, z), f32)],
    )(core_id, weights, *arrays)


def swap(value, axis, distance=1):
    return lax.ppermute(value, axis, [(i, i ^ distance) for i in range(lax.axis_size(axis))])


def local(core_tensor, first_factor, second_factor, third_factor):
    n_gx, n_gy, n_gz = (lax.axis_size(axis) for axis in ("gx", "gy", "gz"))
    gx, gy, gz = (lax.axis_index(axis) for axis in ("gx", "gy", "gz"))
    _, a, b, g = core_tensor.shape
    half = first_factor.shape[0] // 2
    y, z = second_factor.shape[0], third_factor.shape[0]
    relay = n_gx == 4

    mine_first = jnp.where(gz == 0, first_factor, jnp.roll(first_factor, half, axis=0))
    f1 = jnp.concatenate([mine_first] + [swap(mine_first, "gx", k) for k in range(1, n_gx)], axis=0)
    f1 = lax.dynamic_slice_in_dim(f1, gx * a, a, axis=1)

    padded = jnp.zeros((n_gy * y + 4, second_factor.shape[1]), f32)
    for k in range(n_gy):
        block = second_factor if k == 0 else swap(second_factor, "gy", k)
        padded = lax.dynamic_update_slice(padded, block, ((gy ^ k) * y + 2, 0))
    f2 = lax.dynamic_slice_in_dim(padded, gy * y, y + 4, axis=0)
    f2 = jnp.concatenate([f2[2:], jnp.zeros((4, f2.shape[1]), f32), f2[:2]], axis=0)
    f2 = jnp.concatenate(
        [
            lax.dynamic_slice_in_dim(f2, ((gy ^ k) * n_gz + (gz ^ j)) * b, b, axis=1)
            for k in range(n_gy)
            for j in range(n_gz)
        ],
        axis=1,
    )

    edge = swap(jnp.where(gz == 0, third_factor[-2:], third_factor[:2]), "gz")
    extended = jnp.concatenate(
        [jnp.where(gz == 0, 0.0, edge), third_factor, jnp.where(gz == 0, edge, 0.0)], axis=0
    )
    slope = 8.0 * (extended[3:-1] - extended[1:-3]) - (extended[4:] - extended[:-4])
    weights = jnp.concatenate([third_factor, slope], axis=0).T / 12.0

    core = core_tensor.reshape(3 * a * b, g)
    middle = (gx == 1) | (gx == 2)
    owned, partner, arrived, passed = [], [], [], []
    for c in range(3):
        mine, theirs, *sends = expand_first(c, f1, core, a, b, half, relay)
        if relay:
            near, far, cross = sends
            near = swap(near, "gx", 1)
            far = (far + jnp.where(middle, near[1].astype(f32), 0.0)).astype(bf16)
            cross = lax.ppermute(cross, "gx", [(1, 2), (2, 1)])
            got = [near, swap(far, "gx", 2), cross]
        else:
            got = [swap(send, "gx", k + 1) for k, send in enumerate(sends)]
        mine, theirs = add(half, mine, theirs, got)
        other = swap(theirs, "gz")
        away = jnp.concatenate([mine, other], axis=0).astype(bf16)
        others = [swap(away, "gy", k) for k in range(1, n_gy)]
        two = expand_second(half, f2, mine, other, others)
        edge = jnp.where(gz == 0, two[: 2 * (y + 8)], two[-2 * (y + 8) :]).astype(bf16)
        pairs = [(2 * i, 2 * i - 2) for i in range(1, n_gx)] + [(2 * i + 1, 2 * i + 3) for i in range(n_gx - 1)]
        edge = lax.ppermute(edge, ("gx", "gz"), pairs)
        owned.append(two)
        partner.append(swap(two, "gz"))
        arrived.append(edge)
        passed.append(swap(edge, "gz"))
    core_id = gz.astype(jnp.int32).reshape(1)
    curl, q = finish(half, y, z, core_id, weights, owned, partner, arrived, passed)
    return curl, q


def solution(mesh):
    return jax.shard_map(
        local,
        mesh=mesh,
        in_specs=(
            P(None, ("snap", "gx"), ("gy", "gz"), None),
            P(("snap", "gx"), None),
            P(("snap", "gy"), None),
            P(("snap", "gz"), None),
        ),
        out_specs=(P(None, ("snap", "gx"), "gy", "gz"), P(("snap", "gx"), "gy", "gz")),
        check_vma=False,
    )
```

```python
import functools

import jax
import jax.numpy as jnp
from jax import lax
from jax.experimental import pallas as pl
from jax.experimental.pallas import tpu as pltpu
from jax.sharding import PartitionSpec as P

f32, bf16 = jnp.float32, jnp.bfloat16
LANES = 128


def split(value):
    high = value.astype(bf16)
    return high, (value - high.astype(f32)).astype(bf16)


def dot(left, right):
    return jnp.dot(left, right, preferred_element_type=f32)


def whole(shape):
    return pl.BlockSpec(shape, lambda *_: (0,) * len(shape))


HBM = pl.BlockSpec(memory_space=pltpu.HBM)
ANY = pl.BlockSpec(memory_space=pl.ANY)
SCALARS = pl.BlockSpec(memory_space=pltpu.SMEM)


def call(kernel, outs, inputs, scratch=(), specs=None, after=(), vmem=16, alias=None, out_specs=None, us=0):
    specs = [whole(x.shape) for x in inputs] if specs is None else specs
    count = len(inputs)

    def body(*refs):
        kernel(*refs[:count], *refs[count + len(after) :])

    return pl.pallas_call(
        body,
        grid=(1,),
        out_shape=outs,
        in_specs=specs + [ANY] * len(after),
        out_specs=out_specs or jax.tree.map(lambda s: whole(s.shape), outs),
        scratch_shapes=scratch,
        input_output_aliases=alias or {},
        compiler_params=pltpu.CompilerParams(vmem_limit_bytes=vmem * 2**20),
        cost_estimate=pl.CostEstimate(flops=us * 10**9 + 1, bytes_accessed=us * 4 * 10**6 + 1, transcendentals=0),
    )(*inputs, *after)


def struct(*shape, dtype=f32):
    return jax.ShapeDtypeStruct(shape, dtype)


def unfold_kernel(core, out, buffer, arrived):
    _, pieces, a, chunk, _ = buffer.shape
    copies = [
        [
            pltpu.make_async_copy(
                core.at[c, :, pl.ds(i * chunk, chunk), :], buffer.at[c, i], arrived.at[c, i]
            )
            for i in range(pieces)
        ]
        for c in range(3)
    ]
    for row in copies:
        for copy in row:
            copy.start()
    for c in range(3):
        for i in range(pieces):
            copies[c][i].wait()
            view = buffer.at[c, i].reshape(a * chunk, LANES)
            for j in range(0, chunk, 2):
                pair = jnp.concatenate(
                    [view[pl.ds(j + q, a, stride=chunk), :] for q in range(2)], axis=1
                )
                high, low = split(pair)
                out[c, (i * chunk + j) // 2, :a, :] = high
                out[c, (i * chunk + j) // 2, a:, :] = low


def unfold(core):
    _, a, b, _ = core.shape
    chunk = min(b, 16)
    return call(
        unfold_kernel,
        struct(3, b // 2, 2 * a, 2 * LANES, dtype=bf16),
        [pltpu.with_memory_space_constraint(core, pltpu.HBM)],
        [pltpu.VMEM((3, b // chunk, a, chunk, LANES), f32), pltpu.SemaphoreType.DMA((3, b // chunk))],
        [HBM],
        vmem=24,
    )


def expand_first_kernel(n, relayed, counts, ids, *refs):
    factors, core, outs = refs[:n], refs[n], refs[n + 1 :]
    gx, gz = ids[0], ids[2]
    a = core.shape[2] // 2
    rows = []
    for ref in factors:
        half = ref.shape[0] // 2
        top, bottom = ref[:half, :], ref[half:, :]
        rows += [jnp.where(gz == 0, top, bottom), jnp.where(gz == 0, bottom, top)]
    f1 = exchange_columns(jnp.concatenate(rows, axis=0), gx, a, n)[:, :a]
    high, low = split(f1)
    left = jnp.concatenate([high, high, low], axis=1)
    for c in range(3):
        mine = outs[sum(counts[:c]) : sum(counts[: c + 1])]
        for pair in range(core.shape[1]):
            right = core[c, pair]
            out = dot(left, jnp.concatenate([right, right[:a]], axis=0))
            for q in range(2):
                column = out[:, q * LANES : (q + 1) * LANES]
                if c == 2:
                    store_halves(half, 2 * pair + q, column, *mine)
                else:
                    store_blocks(half, 2 * pair + q, column, relayed[c], *mine)


def exchange_columns(value, index, size, count):
    width = value.shape[1]
    column = lax.broadcasted_iota(jnp.int32, value.shape, 1)
    step = 1
    while step < count:
        reach = step * size
        other = jnp.where(
            (column // reach) % 2 == 0,
            pltpu.roll(value, width - reach, 1),
            pltpu.roll(value, reach, 1),
        )
        value = jnp.where((index // step) % 2 == 1, other, value)
        step *= 2
    return value


def rows_at(index, size):
    return pl.ds(index * size, size)


def store_sends(full, block, relayed, sends):
    if relayed:
        near, far, cross = sends
        near[0, full, :] = block[1].astype(bf16)
        near[1, full, :] = block[3].astype(bf16)
        far[full, :] = block[2]
        cross[full, :] = block[3].astype(bf16)
    else:
        for k, send in enumerate(sends):
            send[full, :] = block[k + 1].astype(bf16)


def sends_of(n, rows, relayed):
    full = struct(rows, LANES, dtype=bf16)
    if relayed:
        return [struct(2, rows, LANES, dtype=bf16), struct(rows, LANES), full]
    return [full] * (n - 1)


def store_blocks(half, b_index, rows, relayed, mine, theirs, *sends):
    short, full = rows_at(b_index, half), rows_at(b_index, 2 * half)
    mine[short, :] = rows[:half]
    theirs[short, :] = rows[half : 2 * half]
    n = rows.shape[0] // (2 * half)
    block = [rows[2 * half * k : 2 * half * (k + 1)] for k in range(n)]
    store_sends(full, block, relayed, sends)


def store_halves(half, b_index, rows, mine, theirs):
    short = rows_at(b_index, half)
    for k in range(rows.shape[0] // (2 * half)):
        mine[k, short, :] = rows[2 * half * k : 2 * half * k + half]
        theirs[k, short, :] = rows[2 * half * k + half : 2 * half * (k + 1)]


def expand_first(ids, factors, core, half, relayed, after=(), us=0):
    b, n = 2 * core.shape[1], len(factors)
    parts = [[struct(b * half, LANES)] * 2 + sends_of(n, 2 * b * half, relayed[c]) for c in range(2)]
    parts.append([struct(n, b * half, LANES)] * 2)
    outs = call(
        functools.partial(expand_first_kernel, n, relayed, [len(x) for x in parts]),
        sum(parts, []),
        [ids, *factors, core],
        specs=[SCALARS] + [whole(x.shape) for x in factors] + [whole(core.shape)],
        after=after,
        vmem=24,
        us=us,
    )
    count = len(parts[0])
    return outs[:count], outs[count:-2], outs[-2:]


def prepare_kernel(n_gy, n_gz, ids, *refs):
    blocks, third, next_third, f2, chip, weights = refs[:n_gy], *refs[n_gy:]
    gy, gz = ids[1], ids[2]
    y, width = blocks[0].shape
    b = width // (n_gy * n_gz)
    row = lax.broadcasted_iota(jnp.int32, (8, width), 0)
    zeros = jnp.zeros((8, width), f32)
    for k in range(n_gy):
        above = below = zeros
        for m in range(n_gy):
            above = jnp.where((gy ^ m) == (gy ^ k) + 1, blocks[m][:8, :], above)
            below = jnp.where((gy ^ m) == (gy ^ k) - 1, blocks[m][y - 8 :, :], below)
        tail = jnp.where(row < 2, above, jnp.where(row >= 6, below, zeros))
        value = jnp.concatenate([blocks[k][...], tail], axis=0)
        value = exchange_columns(exchange_columns(value, gz, b, n_gz), gy, b * n_gz, n_gy)
        if k == 0:
            f2[...] = value
        chip[k * (y + 8) : (k + 1) * (y + 8), :] = value[:, : b * n_gz]
    first, last = next_third[:2, :], next_third[third.shape[0] - 2 :, :]
    none = jnp.zeros_like(first)
    long = jnp.concatenate(
        [jnp.where(gz == 0, none, last), third[...], jnp.where(gz == 0, first, none)], axis=0
    )
    slope = 8.0 * (long[3:-1] - long[1:-3]) - (long[4:] - long[:-4])
    value = jnp.concatenate([third[...].T, slope.T], axis=1) * (1.0 / 12.0)
    high, low = split(value)
    weights[...] = jnp.concatenate([high, high, low], axis=0)


def prepare(ids, blocks, third, next_third, n_gz, after):
    y, width = blocks[0].shape
    n_gy = len(blocks)
    inputs = [ids, *blocks, third, next_third]
    return call(
        functools.partial(prepare_kernel, n_gy, n_gz),
        [
            struct(y + 8, width),
            struct(n_gy * (y + 8), width // n_gy),
            struct(3 * third.shape[1], 2 * third.shape[0], dtype=bf16),
        ],
        inputs,
        specs=[SCALARS] + [whole(x.shape) for x in inputs[1:]],
        after=after,
    )


def relay_kernel(ids, far, near, out):
    middle = (ids[0] == 1) | (ids[0] == 2)
    out[...] = (far[...] + jnp.where(middle, near[0].astype(f32), 0.0)).astype(bf16)


def relay(ids, far, near, after):
    second = pl.BlockSpec((1, *near.shape[1:]), lambda *_: (1, 0, 0))
    return call(
        relay_kernel,
        struct(*far.shape, dtype=bf16),
        [ids, far, near],
        specs=[SCALARS, whole(far.shape), second],
        after=after,
    )


def add_kernel(half, mine, theirs, *refs):
    arrived, (mine_out, theirs_out) = refs[:-2], refs[-2:]
    b = mine.shape[0] // half
    total = 0.0
    for ref in arrived:
        total = total + (ref[0] if len(ref.shape) == 3 else ref[...]).astype(f32)
    total = total.reshape(b, 2, half, LANES)
    mine_out[...] = mine[...] + total[:, 0].reshape(b * half, LANES)
    theirs_out[...] = theirs[...] + total[:, 1].reshape(b * half, LANES)


def block_of(x, index=0):
    return pl.BlockSpec((1, *x.shape[1:]), lambda *_: (index, 0, 0)) if x.ndim == 3 else whole(x.shape)


def add(half, mine, theirs, arrived, after):
    return call(
        functools.partial(add_kernel, half),
        [struct(*mine.shape)] * 2,
        [mine, theirs, *arrived],
        specs=[whole(mine.shape)] * 2 + [block_of(x) for x in arrived],
        after=after,
    )


def expand_second_kernel(half, f2, mine, other, *refs):
    others, out, wide = refs[:-2], refs[-2], refs[-1]
    b = mine.shape[0] // half
    for i, ref in enumerate(others):
        wide[i] = ref[...].astype(f32)
    f2_high, f2_low = split(f2[...])
    y = f2.shape[0]
    for x in range(0, half, 2):
        def columns(ref, length, *index):
            return jnp.concatenate(
                [ref[(*index, pl.ds(x + i, length, stride=half), slice(None))] for i in range(2)], axis=1
            )

        near = jnp.concatenate([columns(mine, b), columns(other, b)], axis=0)
        high, low = split(near)
        far = [columns(wide, 2 * b, i).astype(bf16) for i in range(len(others))]
        every = jnp.concatenate([high, *far], axis=0)
        value = dot(f2_high, every) + dot(f2_low, every) + dot(f2_high[:, : 2 * b], low)
        for i in range(2):
            out[(x + i) * y : (x + i + 1) * y, :] = value[:, i * LANES : (i + 1) * LANES]


def expand_second(half, f2, mine, other, others, after):
    return call(
        functools.partial(expand_second_kernel, half),
        struct(half * f2.shape[0], LANES),
        [f2, mine, other, *others],
        [pltpu.VMEM((max(len(others), 1), 2 * mine.shape[0], LANES), f32)],
        after=after,
    )


def expand_both_kernel(half, pieces, f2, mine, other, own, *away):
    f2_high, f2_low = split(f2[...])
    n, rows = mine.shape[0], own.shape[1] // half
    b = mine.shape[1] // half
    left = jnp.concatenate([f2_high, f2_high, f2_low], axis=1)
    for k in range(n):
        for x in range(0, half, 2):
            pair = [
                jnp.concatenate([ref[k, pl.ds(x + i, b, stride=half), :] for ref in (mine, other)], axis=0)
                for i in range(2)
            ]
            high, low = split(jnp.concatenate(pair, axis=1))
            value = dot(left, jnp.concatenate([high, low, high], axis=0))
            for i in range(2):
                at = slice((x + i) * rows, (x + i + 1) * rows)
                column = value[:, i * LANES : (i + 1) * LANES]
                own[k, at, :] = column[:rows]
                for j in range(len(away) // pieces):
                    part = column[(j + 1) * rows : (j + 2) * rows].astype(bf16)
                    away[j * pieces + k * pieces // n][k % (n // pieces), at, :] = part


def expand_both(half, pieces, f2, mine, other, n_gy, after):
    n, rows = mine.shape[0], half * f2.shape[0] // n_gy
    return call(
        functools.partial(expand_both_kernel, half, pieces),
        [struct(n, rows, LANES)] + [struct(n // pieces, rows, LANES, dtype=bf16)] * (pieces * (n_gy - 1)),
        [f2, mine, other],
        after=after,
        vmem=32,
    )


def sort_second_kernel(count, pieces, relayed, own, *refs):
    others, kept, sends = refs[:count], refs[count], refs[count + 1 :]
    n, rows = own.shape[0], own.shape[1]
    step = rows // 2
    for part in range(2):
        at = pl.ds(part * step, step)
        block = []
        for k in range(n):
            total = own[k, at, :]
            for ref in others[k * pieces // n :: pieces]:
                total = total + ref[k % (n // pieces), at, :].astype(f32)
            block.append(total)
        kept[at, :] = block[0]
        store_sends(at, block, relayed, sends)


def sort_second(own, others, pieces, relayed, after):
    n, rows, _ = own.shape
    return call(
        functools.partial(sort_second_kernel, len(others), pieces, relayed),
        [struct(rows, LANES)] + sends_of(n, rows, relayed),
        [own, *others],
        after=after,
        vmem=32,
    )


def sum_second_kernel(own, *refs):
    total = own[...]
    for ref in refs[:-1]:
        total = total + (ref[0] if len(ref.shape) == 3 else ref[...]).astype(f32)
    refs[-1][...] = total


def sum_second(own, arrived, after):
    return call(
        sum_second_kernel,
        struct(*own.shape),
        [own, *arrived],
        specs=[whole(own.shape)] + [block_of(x) for x in arrived],
        after=after,
    )


def planes(right, value, count, z):
    high, low = split(value)
    out = dot(jnp.concatenate([high, low, high], axis=1), right)
    return out.reshape(count, value.shape[0] // count, 2 * z)


def slope(low2, low1, high1, high2):
    return 8.0 * (high1 - low1) - (high2 - low2)


def finish_most_kernel(half, y, z, ids, weights, *refs):
    owned, partner, (arrived, passed) = refs[0:3], refs[3:6], refs[6:8]
    curl, q, outer, y_rest, z_rest, q_rest, v, along_z = refs[8:]
    right = weights[...]
    rows = y + 8
    core = ids[2]

    def place(c, first, out):
        at = pl.ds(first, out.shape[0])
        v[c, at, 8 : 8 + rows, :] = out[:, :, :z]
        v[c, at, 0:8, :] = out[:, y:, :z]

    for c in range(3):
        for source, slot in ((owned, core), (partner, 1 - core)):
            for part in range(2):
                size = half // 2 * rows
                out = planes(right, source[c][part * size : (part + 1) * size, :], half // 2, z)
                first = slot * half + part * (half // 2)
                place(c, first + 2, out)
                along_z[c, pl.ds(first, half // 2), :, :] = out[:, :y, z:]
    place(0, (1 - core) * (2 * half + 2), planes(right, arrived[0].astype(f32), 2, z))
    place(0, core * (2 * half + 2), planes(right, passed[0].astype(f32), 2, z))
    for c in range(2):
        for i in range(4):
            outer[c, i] = v[1 + c, 2 + i, 8 : 8 + y, :]
            outer[c, 4 + i] = v[1 + c, 2 * half - 2 + i, 8 : 8 + y, :]

    def step(x, rest):
        def dx(c):
            return slope(*(v[c, x + i, 8 : 8 + y, :] for i in (0, 1, 3, 4)))

        def dy(c):
            return slope(*(v[c, x + 2, 6 + i : 6 + i + y, :] for i in (0, 1, 3, 4)))

        def dz(c):
            return along_z[c, x, :, :]

        y0, y2, z0, z1 = dy(0), dy(2), dz(0), dz(1)
        curl[0, x] = (y2 - z1).astype(bf16)
        x0, y1, z2 = dx(0), dy(1), dz(2)
        value = -0.5 * (x0 * x0 + y1 * y1 + z2 * z2) - z1 * y2
        if rest is None:
            x1, x2 = dx(1), dx(2)
            curl[1, x] = (z0 - x2).astype(bf16)
            curl[2, x] = (x1 - y0).astype(bf16)
            q[x] = (value - (y0 * x1 + z0 * x2)).astype(bf16)
        else:
            y_rest[rest] = y0
            z_rest[rest] = z0
            q_rest[rest] = value

    pl.loop(2, 2 * half - 2)(lambda x: step(x, None))
    for rest, x in enumerate((0, 1, 2 * half - 2, 2 * half - 1)):
        step(x, rest)


def finish_rest_kernel(half, y, z, ids, weights, outer, y_rest, z_rest, q_rest, arrived, passed, *refs):
    curl, q, v, curl_out, q_out, done = refs[2:]
    core = ids[2]
    right = weights[...]
    for source, slot in ((arrived, 1 - core), (passed, core)):
        for c in range(2):
            v[c, pl.ds(slot * 6, 2)] = planes(right, source[c].astype(f32), 2, z)[:, :y, :z]
    for c in range(2):
        for i in range(4):
            v[c, 2 + i] = outer[c, i]
            v[c, 8 + i] = outer[c, 4 + i]
    for rest, at in enumerate(((0, 1, 3, 4), (1, 2, 4, 5), (8, 9, 11, 6), (9, 10, 6, 7))):
        x1, x2 = (slope(*(v[c, i] for i in at)) for c in range(2))
        y0, z0 = y_rest[rest], z_rest[rest]
        curl_out[0, rest] = (z0 - x2).astype(bf16)
        curl_out[1, rest] = (x1 - y0).astype(bf16)
        q_out[rest] = (q_rest[rest] - (y0 * x1 + z0 * x2)).astype(bf16)
    copies = []
    for i, x in enumerate((0, 2 * half - 2)):
        at, to = pl.ds(2 * i, 2), pl.ds(x, 2)
        copies.append(pltpu.make_async_copy(curl_out.at[0, at], curl.at[1, to], done.at[3 * i]))
        copies.append(pltpu.make_async_copy(curl_out.at[1, at], curl.at[2, to], done.at[3 * i + 1]))
        copies.append(pltpu.make_async_copy(q_out.at[at], q.at[to], done.at[3 * i + 2]))
    for copy in copies:
        copy.start()
    for copy in copies:
        copy.wait()


def finish_most(half, y, z, ids, weights, owned, partner, arrived, passed):
    arrays = [weights, *owned, *partner, arrived, passed]
    outs = [struct(3, 2 * half, y, z, dtype=bf16), struct(2 * half, y, z, dtype=bf16)]
    return call(
        functools.partial(finish_most_kernel, half, y, z),
        [pltpu.HBM(x.shape, bf16) for x in outs] + [struct(2, 8, y, z)] + [struct(4, y, z)] * 3,
        [ids, *arrays],
        [pltpu.VMEM((3, 2 * half + 4, y + 16, z), f32), pltpu.VMEM((3, 2 * half, y, z), f32)],
        [SCALARS] + [whole(x.shape) for x in arrays],
        vmem=32,
        us=5,
    )


def finish_rest(half, y, z, ids, weights, curl, q, rest, arrived, passed):
    arrays = [weights, *rest, arrived, passed]
    outs = [struct(*curl.shape, dtype=bf16), struct(*q.shape, dtype=bf16)]
    return call(
        functools.partial(finish_rest_kernel, half, y, z),
        outs,
        [ids, *arrays, curl, q],
        [
            pltpu.VMEM((2, 12, y, z), f32),
            pltpu.VMEM((2, 4, y, z), bf16),
            pltpu.VMEM((4, y, z), bf16),
            pltpu.SemaphoreType.DMA((6,)),
        ],
        [SCALARS] + [whole(x.shape) for x in arrays] + [ANY, ANY],
        alias={len(arrays) + 1: 0, len(arrays) + 2: 1},
        out_specs=[ANY, ANY],
    )


def hold(value, after):
    def kernel(source, out):
        out[...] = source[...]

    return call(kernel, struct(*value.shape, dtype=value.dtype), [value], after=after)


def swap(value, axis, distance=1):
    return lax.ppermute(value, axis, [(i, i ^ distance) for i in range(lax.axis_size(axis))])


def scatter_start(sends, relayed):
    if relayed:
        near, far, cross = sends
        return [swap(near, "gx", 1), far, lax.ppermute(cross, "gx", [(1, 2), (2, 1)])]
    return [swap(send, "gx", k + 1) for k, send in enumerate(sends)]


def scatter_relay(ids, arrived, relayed, after):
    if not relayed:
        return arrived, after
    near, far, cross = arrived
    far = relay(ids, far, near, after)
    return [near, swap(far, "gx", 2), cross], [far]


def fence(after, us):
    def kernel(out):
        out[...] = jnp.zeros_like(out)

    return call(kernel, struct(8, LANES), [], after=after, us=us)


FENCE_US = 100


def token(value):
    return swap(value[..., :16, :] if value.ndim == 2 else value[0, :16], "gz")


def local(core_tensor, first_factor, second_factor, third_factor):
    n_gx, n_gy, n_gz = (lax.axis_size(axis) for axis in ("gx", "gy", "gz"))
    ids = jnp.stack([lax.axis_index(axis) for axis in ("gx", "gy", "gz")]).astype(jnp.int32)
    gz = lax.axis_index("gz")
    b = core_tensor.shape[2]
    half = first_factor.shape[0] // n_gz
    y, z = second_factor.shape[0], third_factor.shape[0]
    pairs = [(2 * i, 2 * i - 2) for i in range(1, n_gx)] + [(2 * i + 1, 2 * i + 3) for i in range(n_gx - 1)]

    f1 = [first_factor] + [swap(first_factor, "gx", k) for k in range(1, n_gx)]
    f2 = [second_factor] + [swap(second_factor, "gy", k) for k in range(1, n_gy)]
    f3_next = swap(third_factor, "gz")

    relayed = n_gx == 4
    mine, theirs, other = ([None] * 2 for _ in range(3))
    C = CFG
    rel = [r and relayed for r in C["rel"]]
    us = C["us"]
    A = {}
    order = list(C["order"])
    state = {"last": []}

    def edges(values):
        size = 2 * (y + 8)
        edge = jnp.stack([jnp.where(gz == 0, x[:size], x[-size:]).astype(bf16) for x in values])
        return lax.ppermute(edge, ("gx", "gz"), pairs)

    def exchange(c):
        chip = jnp.concatenate([A["mine", c], A["other", c]], axis=0).astype(bf16)
        return [swap(chip, "gy", k) for k in range(1, n_gy)]

    def k1a(last):
        parts = expand_first(ids, f1, unfold(core_tensor), half, rel, [f3_next] + ([*f2[1:]] if C["f2first"] else []), us["k1a"])
        for c in range(2):
            A["mine", c], A["theirs", c], *A["sends", c] = parts[c]
        A["m2"], A["t2"] = parts[2]
        A["fly", 0] = scatter_start(A["sends", 0], rel[0])
        A["fly", 1] = scatter_start(A["sends", 1], rel[1])
        A["o2"] = swap(A["t2"], "gz")
        return A["m2"]

    def prep(last):
        A["f2"], A["chip"], A["w"] = prepare(ids, f2, third_factor, f3_next, n_gz, last)
        return A["w"]

    def both(last):
        A["own2"], *away2 = expand_both(half, C["gy"], A["chip"], A["m2"], A["o2"], n_gy, last)
        A["others2"] = [swap(x, "gy", k // C["gy"] + 1) for k, x in enumerate(away2)]
        return A["own2"]

    def relay_of(c):
        def run(last):
            if not rel[c]:
                return last[0]
            A["fly", c], (out,) = scatter_relay(ids, A["fly", c], rel[c], last)
            return out
        return run

    def add_of(c):
        def run(last):
            A["mine", c], A["theirs", c] = add(half, A["mine", c], A["theirs", c], A["fly", c], last)
            A["other", c] = swap(A["theirs", c], "gz")
            A["away", c] = exchange(c)
            return A["mine", c]
        return run

    def sort(last):
        A["own2"], *sends = sort_second(A["own2"], A["others2"], C["gy"], rel[2], last)
        A["fly", 2] = scatter_start(sends, rel[2])
        return A["own2"]

    def exp_of(c):
        def run(last):
            A["two", c] = expand_second(half, A["f2"], A["mine", c], A["other", c], A["away", c], last)
            if c == 0:
                A["halo0"] = edges([A["two", 0]])
            return A["two", c]
        return run

    def sum2(last):
        A["two", 2] = sum_second(A["own2"], A["fly", 2], last)
        return A["two", 2]

    steps = dict(k1a=k1a, prep=prep, both=both, r0=relay_of(0), r1=relay_of(1), r2=relay_of(2), add0=add_of(0), add1=add_of(1), sort=sort, exp0=exp_of(0), exp1=exp_of(1), sum2=sum2, halo0=lambda last: A["halo0"], cross0=lambda last: A["fly", 0][-1], cross1=lambda last: A["fly", 1][-1], cross2=lambda last: A["fly", 2][-1], oth0=lambda last: A["other", 0], oth1=lambda last: A["other", 1])
    last = []
    for name in order:
        out = steps[name](last)
        if name in ("halo0", "cross0", "cross1", "cross2", "oth0", "oth1"):
            last = last + [out]
            continue
        last = [out]
        if us.get(name, 0) and name != "k1a":
            last = [fence(last, us[name])]
    two = [A["two", c] for c in range(3)]
    partner = [swap(x, "gz") for x in two]
    arrived = edges(two[1:])
    curl, q, *rest = finish_most(half, y, z, ids, A["w"], two, partner, A["halo0"], swap(A["halo0"], "gz"))
    passed = swap(hold(arrived, [rest[0]]), "gz")
    return tuple(finish_rest(half, y, z, ids, A["w"], curl, q, rest, arrived, passed))


CFG = dict(rel=[False, True, True], gy=1, f2first=True, order=["k1a", "prep", "both", "add0", "r1", "sort", "exp0", "add1", "r2", "halo0", "exp1", "sum2"], us=dict(k1a=0))


def solution(mesh):
    return jax.shard_map(
        local,
        mesh=mesh,
        in_specs=(
            P(None, ("snap", "gx"), ("gy", "gz"), None),
            P(("snap", "gx"), None),
            P(("snap", "gy"), None),
            P(("snap", "gz"), None),
        ),
        out_specs=(P(None, ("snap", "gx"), "gy", "gz"), P(("snap", "gx"), "gy", "gz")),
        check_vma=False,
    )
```

```python
import functools

import jax
import jax.numpy as jnp
from jax import lax
from jax.experimental import pallas as pl
from jax.experimental.pallas import tpu as pltpu
from jax.sharding import PartitionSpec as P

f32, bf16 = jnp.float32, jnp.bfloat16
LANES = 128


def split(value):
    high = value.astype(bf16)
    return high, (value - high.astype(f32)).astype(bf16)


def dot(left, right):
    return jnp.dot(left, right, preferred_element_type=f32)


def whole(shape):
    return pl.BlockSpec(shape, lambda *_: (0,) * len(shape))


HBM = pl.BlockSpec(memory_space=pltpu.HBM)
ANY = pl.BlockSpec(memory_space=pl.ANY)
SCALARS = pl.BlockSpec(memory_space=pltpu.SMEM)


def call(kernel, outs, inputs, scratch=(), specs=None, after=(), vmem=16, alias=None, out_specs=None, us=0):
    specs = [whole(x.shape) for x in inputs] if specs is None else specs
    count = len(inputs)

    def body(*refs):
        kernel(*refs[:count], *refs[count + len(after) :])

    return pl.pallas_call(
        body,
        grid=(1,),
        out_shape=outs,
        in_specs=specs + [ANY] * len(after),
        out_specs=out_specs or jax.tree.map(lambda s: whole(s.shape), outs),
        scratch_shapes=scratch,
        input_output_aliases=alias or {},
        compiler_params=pltpu.CompilerParams(vmem_limit_bytes=vmem * 2**20),
        cost_estimate=pl.CostEstimate(flops=us * 10**9 + 1, bytes_accessed=us * 4 * 10**6 + 1, transcendentals=0),
    )(*inputs, *after)


def struct(*shape, dtype=f32):
    return jax.ShapeDtypeStruct(shape, dtype)


def vmem_struct(*shape, dtype=f32):
    return pltpu.VMEM(shape, dtype)


def unfold_kernel(core, out, buffer, arrived):
    _, pieces, a, chunk, _ = buffer.shape
    copies = [
        [
            pltpu.make_async_copy(
                core.at[c, :, pl.ds(i * chunk, chunk), :], buffer.at[c, i], arrived.at[c, i]
            )
            for i in range(pieces)
        ]
        for c in range(3)
    ]
    for row in copies:
        for copy in row:
            copy.start()
    for c in range(3):
        for i in range(pieces):
            copies[c][i].wait()
            view = buffer.at[c, i].reshape(a * chunk, LANES)
            for j in range(0, chunk, 2):
                pair = jnp.concatenate(
                    [view[pl.ds(j + q, a, stride=chunk), :] for q in range(2)], axis=1
                )
                high, low = split(pair)
                out[c, (i * chunk + j) // 2, :a, :] = high
                out[c, (i * chunk + j) // 2, a:, :] = low


def unfold(core):
    _, a, b, _ = core.shape
    chunk = min(b, 16)
    return call(
        unfold_kernel,
        struct(3, b // 2, 2 * a, 2 * LANES, dtype=bf16),
        [pltpu.with_memory_space_constraint(core, pltpu.HBM)],
        [pltpu.VMEM((3, b // chunk, a, chunk, LANES), f32), pltpu.SemaphoreType.DMA((3, b // chunk))],
        [HBM],
        vmem=24,
    )


def expand_first_kernel(n, ids, *refs):
    factors, core, outs = refs[:n], refs[n], refs[n + 1 :]
    gx, gz = ids[0], ids[2]
    a = core.shape[2] // 2
    rows = []
    for ref in factors:
        half = ref.shape[0] // 2
        top, bottom = ref[:half, :], ref[half:, :]
        rows += [jnp.where(gz == 0, top, bottom), jnp.where(gz == 0, bottom, top)]
    f1 = exchange_columns(jnp.concatenate(rows, axis=0), gx, a, n)[:, :a]
    high, low = split(f1)
    left = jnp.concatenate([high, high, low], axis=1)
    for c in range(3):
        for pair in range(core.shape[1]):
            right = core[c, pair]
            out = dot(left, jnp.concatenate([right, right[:a]], axis=0))
            for q in range(2):
                column = out[:, q * LANES : (q + 1) * LANES]
                if c == 2:
                    store_halves(half, 2 * pair + q, column, *outs[4:6])
                else:
                    store_blocks(half, c, 2 * pair + q, column, *outs[2 * c : 2 * c + 2], outs[6:])


def exchange_columns(value, index, size, count):
    width = value.shape[1]
    column = lax.broadcasted_iota(jnp.int32, value.shape, 1)
    step = 1
    while step < count:
        reach = step * size
        other = jnp.where(
            (column // reach) % 2 == 0,
            pltpu.roll(value, width - reach, 1),
            pltpu.roll(value, reach, 1),
        )
        value = jnp.where((index // step) % 2 == 1, other, value)
        step *= 2
    return value


def rows_at(index, size):
    return pl.ds(index * size, size)


def sends_of(n, rows, relayed):
    full = struct(rows, LANES, dtype=bf16)
    if relayed:
        return [full, struct(rows, LANES), full]
    return [full] * (n - 1)


def store_sends(full, block, relayed, sends):
    if relayed:
        near, far, cross = sends
        near[full, :] = block[1].astype(bf16)
        far[full, :] = block[2]
        cross[full, :] = block[3].astype(bf16)
    else:
        for k, send in enumerate(sends):
            send[full, :] = block[k + 1].astype(bf16)


def first_sends(n, rows):
    if n == 4:
        return [struct(2, rows, LANES, dtype=bf16)] * 2 + [vmem_struct(rows, LANES)] * 2
    return [struct(rows, LANES, dtype=bf16)] * (2 * (n - 1))


def store_first(full, c, block, sends):
    n = len(block)
    if n == 4:
        near, ends, *far = sends
        near[c, full, :] = block[1].astype(bf16)
        ends[c, full, :] = block[3].astype(bf16)
        far[c][full, :] = block[2]
    else:
        for k in range(1, n):
            sends[c * (n - 1) + k - 1][full, :] = block[k].astype(bf16)


def store_blocks(half, c, b_index, rows, mine, theirs, sends):
    short, full = rows_at(b_index, half), rows_at(b_index, 2 * half)
    mine[short, :] = rows[:half]
    theirs[short, :] = rows[half : 2 * half]
    n = rows.shape[0] // (2 * half)
    store_first(full, c, [rows[2 * half * k : 2 * half * (k + 1)] for k in range(n)], sends)


def store_halves(half, b_index, rows, mine, theirs):
    short = rows_at(b_index, half)
    for k in range(rows.shape[0] // (2 * half)):
        mine[k, short, :] = rows[2 * half * k : 2 * half * k + half]
        theirs[k, short, :] = rows[2 * half * k + half : 2 * half * (k + 1)]


def expand_first(ids, factors, core, half, after=(), us=0):
    b, n = 2 * core.shape[1], len(factors)
    outs = call(
        functools.partial(expand_first_kernel, n),
        [struct(b * half, LANES)] * 4 + [struct(n, b * half, LANES)] * 2 + first_sends(n, 2 * b * half),
        [ids, *factors, core],
        specs=[SCALARS] + [whole(x.shape) for x in factors] + [whole(core.shape)],
        after=after,
        vmem=24,
        us=us,
    )
    return outs[0:4:2], outs[1:4:2], outs[4:6], outs[6:]


def prepare_kernel(n_gy, n_gz, ids, *refs):
    blocks, third, next_third, f2, chip, weights = refs[:n_gy], *refs[n_gy:]
    gy, gz = ids[1], ids[2]
    y, width = blocks[0].shape
    b = width // (n_gy * n_gz)
    row = lax.broadcasted_iota(jnp.int32, (8, width), 0)
    zeros = jnp.zeros((8, width), f32)
    for k in range(n_gy):
        above = below = zeros
        for m in range(n_gy):
            above = jnp.where((gy ^ m) == (gy ^ k) + 1, blocks[m][:8, :], above)
            below = jnp.where((gy ^ m) == (gy ^ k) - 1, blocks[m][y - 8 :, :], below)
        tail = jnp.where(row < 2, above, jnp.where(row >= 6, below, zeros))
        value = jnp.concatenate([blocks[k][...], tail], axis=0)
        value = exchange_columns(exchange_columns(value, gz, b, n_gz), gy, b * n_gz, n_gy)
        if k == 0:
            f2[...] = value
        chip[k * (y + 8) : (k + 1) * (y + 8), :] = value[:, : b * n_gz]
    first, last = next_third[:2, :], next_third[third.shape[0] - 2 :, :]
    none = jnp.zeros_like(first)
    long = jnp.concatenate(
        [jnp.where(gz == 0, none, last), third[...], jnp.where(gz == 0, first, none)], axis=0
    )
    slope = 8.0 * (long[3:-1] - long[1:-3]) - (long[4:] - long[:-4])
    value = jnp.concatenate([third[...].T, slope.T], axis=1) * (1.0 / 12.0)
    high, low = split(value)
    weights[...] = jnp.concatenate([high, high, low], axis=0)


def prepare(ids, blocks, third, next_third, n_gz, after):
    y, width = blocks[0].shape
    n_gy = len(blocks)
    inputs = [ids, *blocks, third, next_third]
    return call(
        functools.partial(prepare_kernel, n_gy, n_gz),
        [
            struct(y + 8, width),
            struct(n_gy * (y + 8), width // n_gy),
            struct(3 * third.shape[1], 2 * third.shape[0], dtype=bf16),
        ],
        inputs,
        specs=[SCALARS] + [whole(x.shape) for x in inputs[1:]],
        after=after,
    )


def relay_kernel(ids, far, near, out):
    middle = (ids[0] == 1) | (ids[0] == 2)
    value = near[0] if len(near.shape) == 3 else near[...]
    out[...] = (far[...] + jnp.where(middle, value.astype(f32), 0.0)).astype(bf16)


def relay(ids, c, far, near, after):
    second = block_of(near, c)
    return call(
        relay_kernel,
        vmem_struct(*far.shape, dtype=bf16),
        [ids, far, near],
        specs=[SCALARS, whole(far.shape), second],
        after=after,
    )


def add_kernel(half, mine, theirs, *refs):
    arrived, (mine_out, theirs_out) = refs[:-2], refs[-2:]
    b = mine.shape[0] // half
    total = 0.0
    for ref in arrived:
        total = total + (ref[0] if len(ref.shape) == 3 else ref[...]).astype(f32)
    total = total.reshape(b, 2, half, LANES)
    mine_out[...] = mine[...] + total[:, 0].reshape(b * half, LANES)
    theirs_out[...] = theirs[...] + total[:, 1].reshape(b * half, LANES)


def block_of(x, index=0):
    return pl.BlockSpec((1, *x.shape[1:]), lambda *_: (index, 0, 0)) if x.ndim == 3 else whole(x.shape)


def add(half, c, mine, theirs, arrived, after):
    return call(
        functools.partial(add_kernel, half),
        [struct(*mine.shape)] * 2,
        [mine, theirs, *arrived],
        specs=[whole(mine.shape)] * 2 + [block_of(x, c) for x in arrived],
        after=after,
    )


def expand_second_kernel(half, f2, mine, other, *refs):
    others, out, wide = refs[:-2], refs[-2], refs[-1]
    b = mine.shape[0] // half
    for i, ref in enumerate(others):
        wide[i] = ref[...].astype(f32)
    f2_high, f2_low = split(f2[...])
    y = f2.shape[0]
    for x in range(0, half, 2):
        def columns(ref, length, *index):
            return jnp.concatenate(
                [ref[(*index, pl.ds(x + i, length, stride=half), slice(None))] for i in range(2)], axis=1
            )

        near = jnp.concatenate([columns(mine, b), columns(other, b)], axis=0)
        high, low = split(near)
        far = [columns(wide, 2 * b, i).astype(bf16) for i in range(len(others))]
        every = jnp.concatenate([high, *far], axis=0)
        value = dot(f2_high, every) + dot(f2_low, every) + dot(f2_high[:, : 2 * b], low)
        for i in range(2):
            out[(x + i) * y : (x + i + 1) * y, :] = value[:, i * LANES : (i + 1) * LANES]


def expand_second(half, f2, mine, other, others, after):
    return call(
        functools.partial(expand_second_kernel, half),
        struct(half * f2.shape[0], LANES),
        [f2, mine, other, *others],
        [pltpu.VMEM((max(len(others), 1), 2 * mine.shape[0], LANES), f32)],
        after=after,
    )


def expand_both_kernel(half, pieces, f2, mine, other, own, *away):
    f2_high, f2_low = split(f2[...])
    n, rows = mine.shape[0], own.shape[1] // half
    b = mine.shape[1] // half
    left = jnp.concatenate([f2_high, f2_high, f2_low], axis=1)
    for k in range(n):
        for x in range(0, half, 2):
            pair = [
                jnp.concatenate([ref[k, pl.ds(x + i, b, stride=half), :] for ref in (mine, other)], axis=0)
                for i in range(2)
            ]
            high, low = split(jnp.concatenate(pair, axis=1))
            value = dot(left, jnp.concatenate([high, low, high], axis=0))
            for i in range(2):
                at = slice((x + i) * rows, (x + i + 1) * rows)
                column = value[:, i * LANES : (i + 1) * LANES]
                own[k, at, :] = column[:rows]
                for j in range(len(away) // pieces):
                    part = column[(j + 1) * rows : (j + 2) * rows].astype(bf16)
                    away[j * pieces + k * pieces // n][k % (n // pieces), at, :] = part


def expand_both(half, pieces, f2, mine, other, n_gy, after):
    n, rows = mine.shape[0], half * f2.shape[0] // n_gy
    return call(
        functools.partial(expand_both_kernel, half, pieces),
        [struct(n, rows, LANES)] + [struct(n // pieces, rows, LANES, dtype=bf16)] * (pieces * (n_gy - 1)),
        [f2, mine, other],
        after=after,
        vmem=32,
    )


def sort_second_kernel(count, pieces, relayed, own, *refs):
    others, kept, sends = refs[:count], refs[count], refs[count + 1 :]
    n, rows = own.shape[0], own.shape[1]
    step = rows // 2
    for part in range(2):
        at = pl.ds(part * step, step)
        block = []
        for k in range(n):
            total = own[k, at, :]
            for ref in others[k * pieces // n :: pieces]:
                total = total + ref[k % (n // pieces), at, :].astype(f32)
            block.append(total)
        kept[at, :] = block[0]
        store_sends(at, block, relayed, sends)


def sort_second(own, others, pieces, relayed, after):
    n, rows, _ = own.shape
    return call(
        functools.partial(sort_second_kernel, len(others), pieces, relayed),
        [struct(rows, LANES)] + sends_of(n, rows, relayed),
        [own, *others],
        after=after,
        vmem=32,
    )


def sum_second_kernel(own, *refs):
    total = own[...]
    for ref in refs[:-1]:
        total = total + (ref[0] if len(ref.shape) == 3 else ref[...]).astype(f32)
    refs[-1][...] = total


def sum_second(own, arrived, after):
    return call(
        sum_second_kernel,
        struct(*own.shape),
        [own, *arrived],
        specs=[whole(own.shape)] + [block_of(x) for x in arrived],
        after=after,
    )


def planes(right, value, count, z):
    high, low = split(value)
    out = dot(jnp.concatenate([high, low, high], axis=1), right)
    return out.reshape(count, value.shape[0] // count, 2 * z)


def slope(low2, low1, high1, high2):
    return 8.0 * (high1 - low1) - (high2 - low2)


def finish_most_kernel(half, y, z, ids, weights, *refs):
    owned, partner, (arrived, passed) = refs[0:3], refs[3:6], refs[6:8]
    curl, q, outer, y_rest, z_rest, q_rest, v, along_z = refs[8:]
    right = weights[...]
    rows = y + 8
    core = ids[2]

    def place(c, first, out):
        at = pl.ds(first, out.shape[0])
        v[c, at, 8 : 8 + rows, :] = out[:, :, :z]
        v[c, at, 0:8, :] = out[:, y:, :z]

    for c in range(3):
        for source, slot in ((owned, core), (partner, 1 - core)):
            for part in range(2):
                size = half // 2 * rows
                out = planes(right, source[c][part * size : (part + 1) * size, :], half // 2, z)
                first = slot * half + part * (half // 2)
                place(c, first + 2, out)
                along_z[c, pl.ds(first, half // 2), :, :] = out[:, :y, z:]
    place(0, (1 - core) * (2 * half + 2), planes(right, arrived[0].astype(f32), 2, z))
    place(0, core * (2 * half + 2), planes(right, passed[0].astype(f32), 2, z))
    for c in range(2):
        for i in range(4):
            outer[c, i] = v[1 + c, 2 + i, 8 : 8 + y, :]
            outer[c, 4 + i] = v[1 + c, 2 * half - 2 + i, 8 : 8 + y, :]

    def step(x, rest):
        def dx(c):
            return slope(*(v[c, x + i, 8 : 8 + y, :] for i in (0, 1, 3, 4)))

        def dy(c):
            return slope(*(v[c, x + 2, 6 + i : 6 + i + y, :] for i in (0, 1, 3, 4)))

        def dz(c):
            return along_z[c, x, :, :]

        y0, y2, z0, z1 = dy(0), dy(2), dz(0), dz(1)
        curl[0, x] = (y2 - z1).astype(bf16)
        x0, y1, z2 = dx(0), dy(1), dz(2)
        value = -0.5 * (x0 * x0 + y1 * y1 + z2 * z2) - z1 * y2
        if rest is None:
            x1, x2 = dx(1), dx(2)
            curl[1, x] = (z0 - x2).astype(bf16)
            curl[2, x] = (x1 - y0).astype(bf16)
            q[x] = (value - (y0 * x1 + z0 * x2)).astype(bf16)
        else:
            y_rest[rest] = y0
            z_rest[rest] = z0
            q_rest[rest] = value

    pl.loop(2, 2 * half - 2)(lambda x: step(x, None))
    for rest, x in enumerate((0, 1, 2 * half - 2, 2 * half - 1)):
        step(x, rest)


def finish_rest_kernel(half, y, z, ids, weights, outer, y_rest, z_rest, q_rest, arrived, passed, *refs):
    curl, q, v, curl_out, q_out, done = refs[2:]
    core = ids[2]
    right = weights[...]
    for source, slot in ((arrived, 1 - core), (passed, core)):
        for c in range(2):
            v[c, pl.ds(slot * 6, 2)] = planes(right, source[c].astype(f32), 2, z)[:, :y, :z]
    for c in range(2):
        for i in range(4):
            v[c, 2 + i] = outer[c, i]
            v[c, 8 + i] = outer[c, 4 + i]
    copies = []
    for side, planes_of in enumerate((((0, 1, 3, 4), (1, 2, 4, 5)), ((8, 9, 11, 6), (9, 10, 6, 7)))):
        for i, at in enumerate(planes_of):
            rest = 2 * side + i
            x1, x2 = (slope(*(v[c, j] for j in at)) for c in range(2))
            y0, z0 = y_rest[rest], z_rest[rest]
            curl_out[0, rest] = (z0 - x2).astype(bf16)
            curl_out[1, rest] = (x1 - y0).astype(bf16)
            q_out[rest] = (q_rest[rest] - (y0 * x1 + z0 * x2)).astype(bf16)
        at, to = pl.ds(2 * side, 2), pl.ds(side * (2 * half - 2), 2)
        copies += [
            pltpu.make_async_copy(curl_out.at[0, at], curl.at[1, to], done.at[3 * side]),
            pltpu.make_async_copy(curl_out.at[1, at], curl.at[2, to], done.at[3 * side + 1]),
            pltpu.make_async_copy(q_out.at[at], q.at[to], done.at[3 * side + 2]),
        ]
        for copy in copies[-3:]:
            copy.start()
    for copy in copies:
        copy.wait()


def finish_most(half, y, z, ids, weights, owned, partner, arrived, passed):
    arrays = [weights, *owned, *partner, arrived, passed]
    outs = [struct(3, 2 * half, y, z, dtype=bf16), struct(2 * half, y, z, dtype=bf16)]
    return call(
        functools.partial(finish_most_kernel, half, y, z),
        [pltpu.HBM(x.shape, bf16) for x in outs] + [struct(2, 8, y, z)] + [struct(4, y, z)] * 3,
        [ids, *arrays],
        [pltpu.VMEM((3, 2 * half + 4, y + 16, z), f32), pltpu.VMEM((3, 2 * half, y, z), f32)],
        [SCALARS] + [whole(x.shape) for x in arrays],
        vmem=32,
        us=5,
    )


def finish_rest(half, y, z, ids, weights, curl, q, rest, arrived, passed):
    arrays = [weights, *rest, arrived, passed]
    outs = [struct(*curl.shape, dtype=bf16), struct(*q.shape, dtype=bf16)]
    return call(
        functools.partial(finish_rest_kernel, half, y, z),
        outs,
        [ids, *arrays, curl, q],
        [
            pltpu.VMEM((2, 12, y, z), f32),
            pltpu.VMEM((2, 4, y, z), bf16),
            pltpu.VMEM((4, y, z), bf16),
            pltpu.SemaphoreType.DMA((6,)),
        ],
        [SCALARS] + [whole(x.shape) for x in arrays] + [ANY, ANY],
        alias={len(arrays) + 1: 0, len(arrays) + 2: 1},
        out_specs=[ANY, ANY],
    )


def hold(value, after):
    def kernel(source, out):
        out[...] = source[...]

    return call(kernel, vmem_struct(*value.shape, dtype=value.dtype), [value], after=after)


def swap(value, axis, distance=1):
    return lax.ppermute(value, axis, [(i, i ^ distance) for i in range(lax.axis_size(axis))])


def relay_both_kernel(ids, far0, far1, near, out):
    middle = (ids[0] == 1) | (ids[0] == 2)
    for c, far in enumerate((far0, far1)):
        out[c] = (far[...] + jnp.where(middle, near[c].astype(f32), 0.0)).astype(bf16)


def relay_both(ids, far, near, after):
    return call(
        relay_both_kernel,
        vmem_struct(*near.shape, dtype=bf16),
        [ids, *far, near],
        specs=[SCALARS] + [whole(x.shape) for x in (*far, near)],
        after=after,
    )


def scatter_start(sends, relayed):
    if relayed:
        near, far, cross = sends
        return [swap(near, "gx", 1), far, middle_swap(cross), ends_send(cross)]
    return [swap(send, "gx", k + 1) for k, send in enumerate(sends)]


def middle_swap(cross):
    return lax.ppermute(cross, "gx", [(1, 2), (2, 1)])


def ends_send(ends):
    return lax.ppermute(ends, "gx", [(0, 1), (3, 2)])


def scatter_relay(ids, c, arrived, relayed, after):
    if not relayed:
        return arrived, after
    near, far, cross, ends = arrived
    far = relay(ids, c, far, ends, after)
    return [near, swap(far, "gx", 2), cross], [far]


def fence(after, us):
    def kernel(out):
        out[...] = jnp.zeros_like(out)

    return call(kernel, struct(8, LANES), [], after=after, us=us)


FENCE_US = 100


def token(value):
    return swap(value[..., :16, :] if value.ndim == 2 else value[0, :16], "gz")


def local(core_tensor, first_factor, second_factor, third_factor):
    n_gx, n_gy, n_gz = (lax.axis_size(axis) for axis in ("gx", "gy", "gz"))
    ids = jnp.stack([lax.axis_index(axis) for axis in ("gx", "gy", "gz")]).astype(jnp.int32)
    gz = lax.axis_index("gz")
    b = core_tensor.shape[2]
    half = first_factor.shape[0] // n_gz
    y, z = second_factor.shape[0], third_factor.shape[0]
    pairs = [(2 * i, 2 * i - 2) for i in range(1, n_gx)] + [(2 * i + 1, 2 * i + 3) for i in range(n_gx - 1)]

    f1 = [first_factor] + [swap(first_factor, "gx", k) for k in range(1, n_gx)]
    f2 = [second_factor] + [swap(second_factor, "gy", k) for k in range(1, n_gy)]
    f3_next = swap(third_factor, "gz")

    relayed = n_gx == 4
    mine, theirs, other = ([None] * 2 for _ in range(3))
    C = CFG
    rel = [r and relayed for r in C["rel"]]
    us = C["us"]
    A = {}
    order = list(C["order"])
    state = {"last": []}

    def edges(values):
        size = 2 * (y + 8)
        edge = jnp.stack([jnp.where(gz == 0, x[:size], x[-size:]).astype(bf16) for x in values])
        return lax.ppermute(edge, ("gx", "gz"), pairs)

    def exchange(c):
        chip = jnp.concatenate([A["mine", c], A["other", c]], axis=0).astype(bf16)
        return [swap(chip, "gy", k) for k in range(1, n_gy)]

    def k1a(last):
        mine, theirs, (A["m2"], A["t2"]), sends = expand_first(ids, f1, unfold(core_tensor), half, [f3_next] + ([*f2[1:]] if C["f2first"] else []), us["k1a"])
        for c in range(2):
            A["mine", c], A["theirs", c] = mine[c], theirs[c]
        if relayed:
            near, ends, *far = sends
            near, cross, ends = swap(near, "gx", 1), middle_swap(ends), ends_send(ends)
            for c in range(2):
                A["fly", c] = [near, far[c], cross, ends]
        else:
            A["fly", 0] = scatter_start(sends[: n_gx - 1], False)
            A["fly", 1] = scatter_start(sends[n_gx - 1 :], False)
        A["o2"] = swap(A["t2"], "gz")
        return A["m2"]

    def prep(last):
        A["f2"], A["chip"], A["w"] = prepare(ids, f2, third_factor, f3_next, n_gz, last)
        return A["w"]

    def both(last):
        A["own2"], *away2 = expand_both(half, C["gy"], A["chip"], A["m2"], A["o2"], n_gy, last)
        A["others2"] = [swap(x, "gy", k // C["gy"] + 1) for k, x in enumerate(away2)]
        return A["own2"]

    def r0(last):
        if not relayed:
            return last[0]
        out = relay_both(ids, [A["fly", c][1] for c in range(2)], A["fly", 0][3], last)
        far = swap(out, "gx", 2)
        for c in range(2):
            A["fly", c] = [A["fly", c][0], far, A["fly", c][2], A["fly", c][3]]
        return out

    def relay_of(c):
        def run(last):
            if not rel[c]:
                return last[0]
            A["fly", c], (out,) = scatter_relay(ids, c, A["fly", c], rel[c], last)
            return out
        return run

    def add_of(c):
        def run(last):
            A["mine", c], A["theirs", c] = add(half, c, A["mine", c], A["theirs", c], A["fly", c][:3] if rel[c] else A["fly", c], last)
            A["other", c] = swap(A["theirs", c], "gz")
            A["away", c] = exchange(c)
            return A["mine", c]
        return run

    def sort(last):
        A["own2"], *sends = sort_second(A["own2"], A["others2"], C["gy"], rel[2], last)
        A["fly", 2] = scatter_start(sends, rel[2])
        return A["own2"]

    def exp_of(c):
        def run(last):
            A["two", c] = expand_second(half, A["f2"], A["mine", c], A["other", c], A["away", c], last)
            if c == 0:
                A["halo0"] = edges([A["two", 0]])
            return A["two", c]
        return run

    def sum2(last):
        A["two", 2] = sum_second(A["own2"], A["fly", 2][:3] if rel[2] else A["fly", 2], last)
        return A["two", 2]

    steps = dict(k1a=k1a, prep=prep, both=both, r0=r0, r2=relay_of(2), add0=add_of(0), add1=add_of(1), sort=sort, exp0=exp_of(0), exp1=exp_of(1), sum2=sum2, halo0=lambda last: A["halo0"], cross0=lambda last: A["fly", 0][-1], cross1=lambda last: A["fly", 1][2], cross2=lambda last: A["fly", 2][2], oth0=lambda last: A["other", 0], oth1=lambda last: A["other", 1], gy2=lambda last: A["others2"][0], ends01=lambda last: A["fly", 0][3], ends2=lambda last: A["fly", 2][3], nx2=lambda last: A["fly", 2][0], pro1=lambda last: A["two", 1])
    last = []
    for name in order:
        out = steps[name](last)
        if name in ("halo0", "cross0", "cross1", "cross2", "ends01", "oth0", "oth1", "gy2", "ends2", "nx2"):
            last = last + [out]
            continue
        last = [out]
        if us.get(name, 0) and name != "k1a":
            last = [fence(last, us[name])]
    two = [A["two", c] for c in range(3)]
    partner = [swap(x, "gz") for x in two]
    arrived = edges(two[1:])
    curl, q, *rest = finish_most(half, y, z, ids, A["w"], two, partner, A["halo0"], swap(A["halo0"], "gz"))
    passed = swap(hold(arrived, [rest[0]]), "gz")
    return tuple(finish_rest(half, y, z, ids, A["w"], curl, q, rest, arrived, passed))


CFG = dict(
    rel=[True, True, True],
    gy=1,
    f2first=False,
    order=(
        "k1a",
        "prep",
        "both",
        "r0",
        "sort",
        "ends2",
        "add0",
        "add1",
        "cross1",
        "cross2",
        "r2",
        "exp0",
        "halo0",
        "exp1",
        "sum2",
    ),
    us=dict(k1a=4, r0=4, add0=4, prep=25),
)


def solution(mesh):
    return jax.shard_map(
        local,
        mesh=mesh,
        in_specs=(
            P(None, ("snap", "gx"), ("gy", "gz"), None),
            P(("snap", "gx"), None),
            P(("snap", "gy"), None),
            P(("snap", "gz"), None),
        ),
        out_specs=(P(None, ("snap", "gx"), "gy", "gz"), P(("snap", "gx"), "gy", "gz")),
        check_vma=False,
    )
```
